32 devices in a mesh: tok: 4 (over y, core), voc: 8 (over z, x).
Axes of the slice: x: 2, y: 2, z: 4, core: 2. Of those that a mesh axis runs over, the one named last changes fastest.
Arguments:
- hidden: bfloat16 [512, 2880], P('tok'), may hold values from -40 to 40
- frozen_head_weight: bfloat16 [2880, 201088], P(None, ('tok', 'voc')), may hold values from -2 to 2
- adapter_down: bfloat16 [2880, 32], replicated, may hold values from -1 to 1
- adapter_up: bfloat16 [32, 201088], P(None, ('tok', 'voc')), may hold values from -1.5 to 1.5
- targets: int32 [512], P('tok'), may hold values from 0 to 201087
- segment: int32 [512], P('tok'), may hold values from 0 to 15, as said below
- response: int32 [512], P('tok'), may hold values from 0 to 1, as said below
- chosen_first: int32 [8], replicated, may hold values 0 or 1
- reference_logp: float32 [16], replicated, may hold values from -20 to -17
Outputs:
- log_ratio: float32 [16], replicated
- hidden_gradient: bfloat16 [512, 2880], P('tok', 'voc')
- adapter_down_gradient: float32 [2880, 32], replicated
- adapter_up_gradient: float32 [32, 201088], P(None, ('tok', 'voc'))
The draws below stay inside these ranges and needn't reach their ends.
Inputs may be any that keep to these rules, and one draw needn't show every extreme that they name: `segment`: sequence numbers never fall; every sequence has an even length of 2 or more; the rows of one index of tok hold exactly 4 whole sequences; sequences 2p and 2p+1 form pair p. The response rows of a sequence are its last rows, 1 to half of its length of them; the rows of one index of tok hold at most 64 response rows, and some index holds exactly 64.
All inputs are finite; a program needn't handle non-finite values.
Results may differ from the reference program's by a relative error of at most 0.0072.
Values may be sent and summed in bfloat16 or wider, within the bound.
A program may use at most 128 MiB of HBM per device.

```python
import math
import jax
import jax.numpy as jnp
import numpy as np
from jax import lax

MODEL_WIDTH = 2880
VOCAB_SIZE = 201088
ADAPTER_RANK = 32
TOK_DEV = 128
SEQ_DEV = 4
PACKED_ROWS = 512
NSEQ = 16
NPAIR = 8


def head_column(key, block_index):
    column_key = jax.random.fold_in(jax.random.fold_in(key, 11), block_index)
    values = jax.random.normal(column_key, (MODEL_WIDTH,), jnp.float32) * (3.0 / math.sqrt(MODEL_WIDTH))
    return jnp.clip(values, -2.0, 2.0)


def adapter_up_column(key, block_index):
    column_key = jax.random.fold_in(jax.random.fold_in(key, 13), block_index)
    values = jax.random.normal(column_key, (ADAPTER_RANK,), jnp.float32) / math.sqrt(ADAPTER_RANK)
    return jnp.clip(values, -1.5, 1.5)


def adapter_a_values(key):
    values = jax.random.normal(jax.random.fold_in(key, 12), (MODEL_WIDTH, ADAPTER_RANK), jnp.float32) / math.sqrt(MODEL_WIDTH)
    return jnp.clip(values, -1.0, 1.0)


def draw_frozen_head_weight(key, part):
    columns = jax.vmap(lambda block_index: head_column(key, block_index), out_axes=1)(jnp.arange(VOCAB_SIZE, dtype=jnp.int32))
    return columns.astype(jnp.bfloat16)


def draw_adapter_down(key, part):
    return adapter_a_values(key).astype(jnp.bfloat16)


def draw_adapter_up(key, part):
    columns = jax.vmap(lambda block_index: adapter_up_column(key, block_index), out_axes=1)(jnp.arange(VOCAB_SIZE, dtype=jnp.int32))
    return columns.astype(jnp.bfloat16)


def draw_hidden(key, part):
    hidden_key = jax.random.fold_in(key, 14)
    values = jnp.clip(jax.random.normal(hidden_key, (PACKED_ROWS, MODEL_WIDTH), jnp.float32), -6.0, 6.0)
    return jnp.clip(values, -40.0, 40.0).astype(jnp.bfloat16)


def layout(key):
    base_key = jax.random.fold_in(key, 21)
    block_list = PACKED_ROWS // TOK_DEV
    full_block = jax.random.randint(jax.random.fold_in(base_key, 1), (), 0, block_list)

    def one_block(block_index):
        block_key = jax.random.fold_in(base_key, block_index + 2)
        cut_key, resp_key = jax.random.split(block_key)
        shuffled = jax.random.permutation(cut_key, TOK_DEV // 2 - 1)
        cuts = jnp.sort(2 * (shuffled[:SEQ_DEV - 1] + 1)).astype(jnp.int32)
        starts = jnp.concatenate([jnp.zeros((1,), jnp.int32), cuts])
        ends = jnp.concatenate([cuts, jnp.full((1,), TOK_DEV, jnp.int32)])
        halves = (ends - starts) // 2
        answer_len = jax.random.randint(resp_key, (SEQ_DEV,), 1, halves + 1).astype(jnp.int32)
        answer_len = jnp.where(block_index == full_block, halves, answer_len)
        position = jnp.arange(TOK_DEV, dtype=jnp.int32)
        local = jnp.sum((position[:, None] >= cuts[None, :]).astype(jnp.int32), axis=1).astype(jnp.int32)
        segment_ids = block_index * SEQ_DEV + local
        tail = ends[local] - answer_len[local]
        answer = (position >= tail).astype(jnp.int32)
        return (segment_ids.astype(jnp.int32), answer)
    segment_ids, answer = jax.vmap(one_block)(jnp.arange(block_list, dtype=jnp.int32))
    return (segment_ids.reshape(-1), answer.reshape(-1))


def draw_segment(key, part):
    return layout(key)[0]


def draw_response(key, part):
    return layout(key)[1]


def place_ends(entries, rng, smallest, top_value):
    place = [jax.random.randint(jax.random.fold_in(rng, axis), (), 0, length) for axis, length in enumerate(entries.shape)]
    widest = entries.shape.index(max(entries.shape))
    next_to = place[:widest] + [(place[widest] + 1) % entries.shape[widest]] + place[widest + 1:]
    return entries.at[tuple(place)].set(smallest).at[tuple(next_to)].set(top_value)


def wide_ids(own_key, dims, count, lean):
    loads = [min(1 << octave, count + 1 - (1 << octave)) * (1 << 20) // math.isqrt((1 << octave) ** lean) + 1 for octave in range((count + 1).bit_length()) if 1 << octave <= count]
    scale = 1 + sum(loads) // (1 << 30)
    table = np.cumsum(np.array([max(1, weight // scale) for weight in loads]))
    ticket = jax.random.randint(jax.random.fold_in(own_key, 1), dims, 0, int(table[len(loads) - 1]))
    start = jnp.left_shift(1, jnp.searchsorted(jnp.asarray(table, jnp.int32), ticket, side="right").astype(jnp.int32))
    grade = start - 1 + jax.random.randint(jax.random.fold_in(own_key, 4), dims, 0, 1 << 30) % jnp.minimum(start, count + 1 - start)
    return jax.random.permutation(jax.random.fold_in(own_key, 2), count)[grade].astype(jnp.int32)


def setup_inputs(seed: int = 0) -> dict:
    seeds = jax.random.split(jax.random.key(seed), 10)
    return {
        "hidden": draw_hidden(jax.random.fold_in(seeds[9], 71), 0),
        "frozen_head_weight": draw_frozen_head_weight(jax.random.fold_in(seeds[9], 71), 0),
        "adapter_down": draw_adapter_down(jax.random.fold_in(seeds[9], 71), 0),
        "adapter_up": draw_adapter_up(jax.random.fold_in(seeds[9], 71), 0),
        "targets": place_ends(wide_ids(seeds[4], (PACKED_ROWS,), VOCAB_SIZE, 2), jax.random.fold_in(seeds[4], 3), 0, VOCAB_SIZE - 1).astype(jnp.int32),
        "segment": draw_segment(jax.random.fold_in(seeds[9], 71), 0),
        "response": draw_response(jax.random.fold_in(seeds[9], 71), 0),
        "chosen_first": place_ends((jax.random.randint(seeds[7], (NPAIR,), 0, 2) < 1).astype(jnp.int32), jax.random.fold_in(seeds[7], 1), 0, 1),
        "reference_logp": jnp.clip(jax.random.uniform(seeds[8], (NSEQ,), jnp.float32, -20.0, -17.0), -20.0, -17.0),
    }


adapter_scale = 2.0
target_margin = 10.0


def contract_dims(left, right, left_dim, right_dim):
    return lax.dot_general(left, right, (((left_dim,), (right_dim,)), ((), ())), preferred_element_type=jnp.float32)


def reference(hidden, frozen_head_weight, adapter_down, adapter_up, targets, segment, response, chosen_first, reference_logp):
    current_block = math.gcd(PACKED_ROWS, 128)
    block_list = PACKED_ROWS // current_block
    adapter_input = jnp.dot(hidden, adapter_down, preferred_element_type=jnp.float32).astype(jnp.bfloat16)
    hidden_state_blocks = hidden.reshape(block_list, current_block, MODEL_WIDTH)
    adapter_blocks = adapter_input.reshape(block_list, current_block, ADAPTER_RANK)
    target_token_blocks = targets.reshape(block_list, current_block)

    def logits_per_row(row_count, adapter_rows):
        return jnp.dot(row_count, frozen_head_weight, preferred_element_type=jnp.float32) + adapter_scale * jnp.dot(adapter_rows, adapter_up, preferred_element_type=jnp.float32)

    def forward_pass(input_tuple):
        row_count, adapter_rows, wanted_logits = input_tuple
        logit_matrix = logits_per_row(row_count, adapter_rows)
        peak = jnp.max(logit_matrix, axis=1, keepdims=True)
        log_partition = peak[:, 0] + jnp.log(jnp.sum(jnp.exp(logit_matrix - peak), axis=1))
        picked = jnp.take_along_axis(logit_matrix, wanted_logits[:, None].astype(jnp.int32), axis=1)[:, 0]
        return picked - log_partition, log_partition

    token_log_probability, log_partition = lax.map(forward_pass, (hidden_state_blocks, adapter_blocks, target_token_blocks))
    token_log_probability = token_log_probability.reshape(-1)
    live = response.astype(jnp.float32)
    counts = jax.ops.segment_sum(live, segment, num_segments=NSEQ)
    totals = jax.ops.segment_sum(token_log_probability * live, segment, num_segments=NSEQ)
    log_ratio = totals / counts - reference_logp
    pairs = log_ratio.reshape(NPAIR, 2)
    first_wins = chosen_first == 1
    margin = jnp.where(first_wins, pairs[:, 0] - pairs[:, 1], pairs[:, 1] - pairs[:, 0])
    slope = 2.0 * (margin - target_margin)
    ratio_grad = jnp.stack([jnp.where(first_wins, slope, -slope), jnp.where(first_wins, -slope, slope)], axis=1).reshape(-1)
    row_weight = live * (ratio_grad / counts)[segment]
    head_weight_blocks = row_weight.reshape(block_list, current_block)

    def backward_pass(loop_carry, input_tuple):
        row_count, adapter_rows, wanted_logits, normalizer_rows, weight_list = input_tuple
        logit_matrix = logits_per_row(row_count, adapter_rows)
        predicted = jnp.exp(logit_matrix - normalizer_rows[:, None])
        hits = (jnp.arange(VOCAB_SIZE, dtype=jnp.int32)[None, :] == wanted_logits[:, None].astype(jnp.int32)).astype(jnp.float32)
        logit_gradient = (weight_list[:, None] * (predicted - hits)).astype(jnp.bfloat16)
        loop_carry = loop_carry + adapter_scale * contract_dims(adapter_rows, logit_gradient, 0, 0)
        head_contribution = contract_dims(logit_gradient, frozen_head_weight, 1, 1)
        adapter_contribution = adapter_scale * contract_dims(logit_gradient, adapter_up, 1, 1)
        return loop_carry, (head_contribution, adapter_contribution)

    adapter_up_gradient, (head_contribution, adapter_contribution) = lax.scan(backward_pass, jnp.zeros((ADAPTER_RANK, VOCAB_SIZE), jnp.float32), (hidden_state_blocks, adapter_blocks, target_token_blocks, log_partition, head_weight_blocks))
    adapter_gradient = adapter_contribution.reshape(PACKED_ROWS, ADAPTER_RANK).astype(jnp.bfloat16)
    adapter_down_gradient = contract_dims(hidden, adapter_gradient, 0, 0)
    hidden_gradient = (head_contribution.reshape(PACKED_ROWS, MODEL_WIDTH) + contract_dims(adapter_gradient, adapter_down, 1, 1)).astype(jnp.bfloat16)
    return (log_ratio, hidden_gradient, adapter_down_gradient, adapter_up_gradient)
```

```python
import functools

import jax
import jax.numpy as jnp
from jax import lax
from jax.experimental import pallas as pl
from jax.experimental.pallas import tpu as pltpu
from jax.sharding import PartitionSpec as P

MESH = pl.DeviceIdType.MESH
f32 = jnp.float32
bf16 = jnp.bfloat16
adapter_scale = 2.0
target_margin = 10.0
CORES = 2
Z_CHIPS = 4
KSTEP = 512
NSTEP = 256
VSTEP = 1024
LANES = 128


def dot_nn(a, b):
    return lax.dot_general(a, b, (((1,), (0,)), ((), ())), preferred_element_type=f32)


def dot_nt(a, b):
    return lax.dot_general(a, b, (((1,), (1,)), ((), ())), preferred_element_type=f32)


def dot_tn(a, b):
    return lax.dot_general(a, b, (((0,), (0,)), ((), ())), preferred_element_type=f32)


def eye_mask(n):
    return lax.broadcasted_iota(jnp.int32, (n, n), 0) == lax.broadcasted_iota(jnp.int32, (n, n), 1)


def to_col(row):
    n = row.shape[1]
    return jnp.sum(jnp.where(eye_mask(n), jnp.broadcast_to(row, (n, n)), 0.0), axis=1, keepdims=True)


def to_row(col):
    n = col.shape[0]
    return jnp.sum(jnp.where(eye_mask(n), jnp.broadcast_to(col, (n, n)), 0.0), axis=0, keepdims=True)


def kernel(
    cfg,
    ht,
    w,
    adt,
    adloc,
    au,
    tgt,
    seg,
    rsp,
    cf,
    refl,
    lr_out,
    hg_out,
    adg_out,
    aug_out,
    wv,
    lg,
    probs,
    xa,
    xl,
    lab,
    st,
    mx,
    sm,
    tm,
    g,
    sb,
    ra,
    tb,
    rb,
    ub,
    rc,
    yb,
    yr,
    lp,
    w_sem,
    xs_sem,
    xr_sem,
    ls_sem,
    lr_sem,
    ss_sem,
    sr_sem,
    as_sem,
    ar_sem,
    bs_sem,
    br_sem,
    cs_sem,
    cr_sem,
    ys_sem,
    yr_sem,
    ps_sem,
    pr_sem,
):
    NT, NV, X, Y, Z, S, V, D, K = cfg
    ND = NT * NV
    R = NT * S
    half = Y * S
    FW = D // NV
    LR = K // X
    tok = lax.axis_index("tok")
    voc = lax.axis_index("voc")
    y, core = tok // CORES, tok % CORES
    z, x = voc // X, voc % X
    me = tok * NV + voc
    sib = y * CORES + (1 - core)
    kst = list(range(0, D, KSTEP))
    nk = len(kst)
    dpad = xa.shape[1]

    def w_copy(i):
        size = min(KSTEP, D - kst[i])
        return pltpu.make_async_copy(
            w.at[pl.ds(kst[i], size), :], wv.at[pl.ds(kst[i], size), :], w_sem.at[i]
        )

    au_copy = pltpu.make_async_copy(au, wv.at[pl.ds(D, K), :], w_sem.at[nk])
    for i in range(nk):
        w_copy(i).start()
    au_copy.start()

    barrier = pltpu.get_barrier_semaphore()

    @pl.loop(1, ND)
    def _(d):
        peer = lax.rem(me + d, ND)
        pl.semaphore_signal(barrier, inc=1, device_id=(peer // NV, peer % NV), device_id_type=MESH)

    rows = ht.shape[1]
    resp = rsp[...]
    tri = (
        lax.broadcasted_iota(jnp.int32, (rows, rows), 0)
        <= lax.broadcasted_iota(jnp.int32, (rows, rows), 1)
    ).astype(bf16)
    before = dot_nn(jnp.broadcast_to(resp.astype(f32), (8, rows)).astype(bf16), tri)[0:1, :]
    position = before.astype(jnp.int32) - 1
    pick = (position == lax.broadcasted_iota(jnp.int32, (S, rows), 0)) & (resp > 0)
    pick_b = pick.astype(f32).astype(bf16)
    myrow = pl.multiple_of(core * half + y * S, S)
    xa[pl.ds(myrow, S), 0:D] = dot_nt(pick_b, ht[...]).astype(bf16)
    if dpad > D:
        xa[pl.ds(myrow, S), D:dpad] = jnp.zeros((S, dpad - D), bf16)
    lane = lax.broadcasted_iota(jnp.int32, (S, LANES), 1)
    t_col = jnp.sum(jnp.where(pick, tgt[...], 0), axis=1, keepdims=True)
    s_col = jnp.sum(jnp.where(pick, seg[...], 0), axis=1, keepdims=True)
    l_col = jnp.sum(jnp.where(pick, 1, 0), axis=1, keepdims=True)
    lab[pl.ds(myrow, S), :] = jnp.where(
        lane == 0, t_col, jnp.where(lane == 1, s_col, jnp.where(lane == 2, l_col, 0))
    )

    pl.semaphore_wait(barrier, ND - 1)

    def x_ref(i, yy, cc):
        size = min(KSTEP, dpad - kst[i])
        r0 = pl.multiple_of(cc * half + yy * S, S)
        return xa.at[pl.ds(r0, S), pl.ds(kst[i], size)]

    def x_copy(i, slot, yy, cc, dev):
        ref = x_ref(i, yy, cc)
        return pltpu.make_async_remote_copy(
            ref, ref, xs_sem.at[i, slot], xr_sem.at[i, slot], device_id=(dev, voc), device_id_type=MESH
        )

    def x_direct(i, dy):
        return x_copy(i, dy, y, core, lax.rem(y + dy, Y) * CORES + core)

    def x_recv(i, slot, yy, cc):
        return x_copy(i, slot, yy, cc, sib)

    def lab_copy(slot, yy, cc, dev):
        r0 = pl.multiple_of(cc * half + yy * S, S)
        ref = lab.at[pl.ds(r0, S), :]
        return pltpu.make_async_remote_copy(
            ref, ref, ls_sem.at[slot], lr_sem.at[slot], device_id=(dev, voc), device_id_type=MESH
        )

    for i in range(nk):
        for dy in range(1, Y):
            x_direct(i, dy).start()
        x_copy(i, 0, y, core, sib).start()
    for d in range(1, NT):
        lab_copy(d, y, core, lax.rem(tok + d, NT)).start()

    def y_from(dy):
        return lax.rem(y + Y - dy, Y)

    def forward(i):
        for dy in range(1, Y):
            x_recv(i, dy, y_from(dy), core).wait_recv()
            x_copy(i, Y - 1 + dy, y_from(dy), core, sib).start()

    def arrive(i):
        x_recv(i, 0, y, 1 - core).wait_recv()
        for dy in range(1, Y):
            x_recv(i, Y - 1 + dy, y_from(dy), 1 - core).wait_recv()

    nfull = V // NSTEP
    vtail = V - nfull * NSTEP
    mx[...] = jnp.full(mx.shape, -jnp.inf, f32)
    sm[...] = jnp.zeros(sm.shape, f32)
    tm[...] = jnp.zeros(tm.shape, f32)

    def folded(tile, op):
        out = tile[:, 0:LANES]
        for j in range(1, NSTEP // LANES):
            out = op(out, tile[:, j * LANES : (j + 1) * LANES])
        return out

    forward(0)
    tail_max = None
    for i in range(nk):
        last = i == nk - 1
        if not last:
            forward(i + 1)
        arrive(i)
        w_copy(i).wait()
        if last:
            size = D - kst[i]
            au_copy.wait()
            acc = dot_nt(xa[:, 0:D], adt[...])
            xl[:, 0:size] = xa[:, kst[i] : D]
            xl[:, size : size + K] = (adapter_scale * acc.astype(bf16).astype(f32)).astype(bf16)
            lhs = xl
            lcols = slice(0, size + K)
            wrows = slice(kst[i], D + K)
        else:
            lhs = xa
            lcols = slice(kst[i], kst[i] + KSTEP)
            wrows = slice(kst[i], kst[i] + KSTEP)

        def step(n, carry, i=i, last=last, lhs=lhs, lcols=lcols, wrows=wrows):
            cols = pl.ds(pl.multiple_of(n * NSTEP, NSTEP), NSTEP)
            tile = dot_nn(lhs[:, lcols], wv[wrows, cols])
            if i > 0:
                tile = tile + lg[:, cols]
            lg[:, cols] = tile
            if last:
                mx[...] = jnp.maximum(mx[...], folded(tile, jnp.maximum))
            return carry

        lax.fori_loop(0, nfull, step, 0)
        if vtail:
            cols = slice(nfull * NSTEP, V)
            tile = dot_nn(lhs[:, lcols], wv[wrows, cols])
            if i > 0:
                tile = tile + lg[:, cols]
            lg[:, cols] = tile
            if last:
                tail_max = jnp.max(tile, axis=1, keepdims=True)

    peak = jnp.max(mx[...], axis=1, keepdims=True)
    if vtail:
        peak = jnp.maximum(peak, tail_max)

    for d in range(1, NT):
        src = lax.rem(tok + NT - d, NT)
        lab_copy(d, src // CORES, src % CORES, sib).wait_recv()
    labels = lab[...]
    target = labels[:, 0:1]
    segs = labels[:, 1:2]
    live = labels[:, 2:3].astype(f32)
    slot_col = jnp.where(live > 0, target - me * V, -1)

    def exp_tile(cols, first, width):
        tile = lg[:, cols]
        hit = (lax.broadcasted_iota(jnp.int32, (R, width), 1) + first) == slot_col
        e = jnp.exp(tile - peak)
        lg[:, cols] = e
        return e, jnp.where(hit, tile, 0.0)

    def exp_step(n, carry):
        cols = pl.ds(pl.multiple_of(n * NSTEP, NSTEP), NSTEP)
        e, t = exp_tile(cols, n * NSTEP, NSTEP)
        sm[...] += folded(e, jnp.add)
        tm[...] += folded(t, jnp.add)
        return carry

    lax.fori_loop(0, nfull, exp_step, 0)
    summed = jnp.sum(sm[...], axis=1, keepdims=True)
    picked = jnp.sum(tm[...], axis=1, keepdims=True)
    if vtail:
        e, t = exp_tile(slice(nfull * NSTEP, V), nfull * NSTEP, vtail)
        summed = summed + jnp.sum(e, axis=1, keepdims=True)
        picked = picked + jnp.sum(t, axis=1, keepdims=True)

    nr = R // LANES
    st[pl.ds(me, 1)] = jnp.zeros((1,) + st.shape[1:], f32)
    for j, col in enumerate((peak, summed, picked)):
        for r in range(nr):
            st[me, j * nr + r : j * nr + r + 1, :] = to_row(col[r * LANES : (r + 1) * LANES, :])

    def st_copy(d, slot):
        peer = lax.rem(me + d, ND)
        return pltpu.make_async_remote_copy(
            st.at[slot],
            st.at[slot],
            ss_sem.at[d],
            sr_sem.at[d],
            device_id=(peer // NV, peer % NV),
            device_id_type=MESH,
        )

    @pl.loop(1, ND)
    def _(d):
        st_copy(d, me).start()

    @pl.loop(1, ND)
    def _(d):
        st_copy(d, lax.rem(me + ND - d, ND)).wait_recv()

    stats = st[...]
    m_all = stats[:, 0:nr, :]
    top = jnp.max(m_all, axis=0)
    total = jnp.sum(stats[:, nr : 2 * nr, :] * jnp.exp(m_all - top[None]), axis=0)
    hit_logit = jnp.sum(stats[:, 2 * nr : 3 * nr, :], axis=0)
    norm = top + jnp.log(total)
    logp = hit_logit - norm
    norm_col = jnp.concatenate([to_col(norm[r : r + 1, :]) for r in range(nr)], axis=0)
    logp_col = jnp.concatenate([to_col(logp[r : r + 1, :]) for r in range(nr)], axis=0)

    nseq = refl.shape[1]
    seq_lane = lax.broadcasted_iota(jnp.int32, (R, LANES), 1)
    mine = (segs == seq_lane) & (live > 0)
    counts = jnp.sum(jnp.where(mine, 1.0, 0.0), axis=0, keepdims=True)
    totals = jnp.sum(jnp.where(mine, logp_col, 0.0), axis=0, keepdims=True)
    counts = jnp.where(counts > 0, counts, 1.0)
    ratio = (totals / counts)[:, 0:nseq] - refl[...]
    lr_out[...] = ratio
    ratio_c = jnp.broadcast_to(ratio, (nseq, nseq))
    si = lax.broadcasted_iota(jnp.int32, (nseq, nseq), 0)
    sj = lax.broadcasted_iota(jnp.int32, (nseq, nseq), 1)
    ratio_col = jnp.sum(jnp.where(si == sj, ratio_c, 0.0), axis=1, keepdims=True)
    other = (si // 2 == sj // 2) & (si != sj)
    ratio_other = jnp.sum(jnp.where(other, jnp.broadcast_to(ratio_col, (nseq, nseq)), 0.0), axis=0, keepdims=True)
    npair = nseq // 2
    pi = lax.broadcasted_iota(jnp.int32, (npair, npair), 0)
    pj = lax.broadcasted_iota(jnp.int32, (npair, npair), 1)
    first_c = jnp.sum(
        jnp.where(pi == pj, jnp.broadcast_to(cf[...], (npair, npair)), 0), axis=1, keepdims=True
    )
    qi = lax.broadcasted_iota(jnp.int32, (npair, nseq), 0)
    qj = lax.broadcasted_iota(jnp.int32, (npair, nseq), 1)
    first = jnp.sum(jnp.where(qi == qj // 2, first_c, 0), axis=0, keepdims=True)
    even = (lax.broadcasted_iota(jnp.int32, (1, nseq), 1) % 2) == 0
    sign = jnp.where((first == 1) == even, 1.0, -1.0)
    margin = sign * (ratio - ratio_other)
    seq_weight = sign * 2.0 * (margin - target_margin) / counts[:, 0:nseq]
    member = (segs == lax.broadcasted_iota(jnp.int32, (R, nseq), 1)) & (live > 0)
    weight = jnp.sum(jnp.where(member, seq_weight, 0.0), axis=1, keepdims=True)
    scale = jnp.exp(peak - norm_col)

    size = D - kst[-1]
    lora = xl[:, size : size + K]
    eye_k = eye_mask(K).astype(f32).astype(bf16)
    lora_t = dot_nt(eye_k, lora).astype(bf16)

    def grad_tile(cols, first_col, width):
        hit = (lax.broadcasted_iota(jnp.int32, (R, width), 1) + first_col) == slot_col
        p = lg[:, cols] * scale
        gr = (weight * jnp.where(hit, p - 1.0, p)).astype(bf16)
        probs[:, cols] = gr
        aug_out[:, cols] = dot_nn(lora_t, gr)

    def grad_step(n, carry):
        grad_tile(pl.ds(pl.multiple_of(n * NSTEP, NSTEP), NSTEP), n * NSTEP, NSTEP)
        return carry

    lax.fori_loop(0, nfull, grad_step, 0)
    if vtail:
        grad_tile(slice(nfull * NSTEP, V), nfull * NSTEP, vtail)

    order = [Z - 1] + list(range(Z - 1))
    vfull = V // VSTEP
    ktail = V - vfull * VSTEP
    CH = X * FW
    F = sb.shape[2]
    keep = pl.multiple_of(core * half, LANES)
    give = pl.multiple_of((1 - core) * half, LANES)

    def product(i):
        q = order[i]
        extra = K if q == Z - 1 else 0
        r0, size = q * CH, CH + extra
        if ktail:
            g[0:size, :] = dot_nt(wv[r0 : r0 + size, vfull * VSTEP : V], probs[:, vfull * VSTEP : V])
        else:
            g[0:size, :] = jnp.zeros((size, R), f32)

        def body(n, carry):
            cols = pl.ds(pl.multiple_of(n * VSTEP, VSTEP), VSTEP)
            g[0:size, :] += dot_nt(wv[r0 : r0 + size, cols], probs[:, cols])
            return carry

        lax.fori_loop(0, vfull, body, 0)
        for xx in range(X):
            sb[i, xx, 0:FW, :] = g[xx * FW : (xx + 1) * FW, :].astype(bf16)
            if extra:
                sb[i, xx, FW : FW + LR, :] = (
                    adapter_scale * g[CH + xx * LR : CH + (xx + 1) * LR, :]
                ).astype(bf16)
                if F > FW + LR:
                    sb[i, xx, FW + LR : F, :] = jnp.zeros((F - FW - LR, R), bf16)
            elif F > FW:
                sb[i, xx, FW:F, :] = jnp.zeros((F - FW, R), bf16)

    def a_copy(i):
        return pltpu.make_async_remote_copy(
            sb.at[i, :, :, pl.ds(give, half)],
            ra.at[i],
            as_sem.at[i],
            ar_sem.at[i],
            device_id=(sib, voc),
            device_id_type=MESH,
        )

    def b_copy(i, dx):
        px = lax.rem(x + dx, X)
        return pltpu.make_async_remote_copy(
            tb.at[i, px],
            rb.at[i, dx - 1],
            bs_sem.at[i, dx],
            br_sem.at[i, dx],
            device_id=(tok, z * X + px),
            device_id_type=MESH,
        )

    def stage_b(i):
        a_copy(i).wait_recv()
        tb[i] = (sb[i, :, :, pl.ds(keep, half)].astype(f32) + ra[i].astype(f32)).astype(bf16)
        for dx in range(1, X):
            b_copy(i, dx).start()

    def c_copy(i, slot):
        return pltpu.make_async_remote_copy(
            ub.at[i],
            rc.at[slot],
            cs_sem.at[i],
            cr_sem.at[slot],
            device_id=(tok, order[i] * X + x),
            device_id_type=MESH,
        )

    def stage_c(i):
        q = order[i]
        total_c = tb[i, x].astype(f32)
        for dx in range(1, X):
            b_copy(i, dx).wait_recv()
            total_c = total_c + rb[i, dx - 1].astype(f32)
        ub[i] = total_c.astype(bf16)

        @pl.when(z != q)
        def _():
            c_copy(i, lax.rem(z + Z - q, Z) - 1).start()

    def y_copy(dy):
        py = lax.rem(y + dy, Y)
        return pltpu.make_async_remote_copy(
            yb.at[py],
            yr.at[dy - 1],
            ys_sem.at[dy],
            yr_sem.at[dy],
            device_id=(py * CORES + core, voc),
            device_id_type=MESH,
        )

    def stage_d(i):
        @pl.when(z == order[i])
        def _():
            total_d = ub[i].astype(f32)
            for j in range(Z - 1):
                pltpu.make_async_remote_copy(
                    ub.at[i],
                    rc.at[j],
                    cs_sem.at[i],
                    cr_sem.at[j],
                    device_id=(sib, voc),
                    device_id_type=MESH,
                ).wait_recv()
                total_d = total_d + rc[j].astype(f32)
            total_d = total_d.astype(bf16)
            for yy in range(Y):
                yb[yy, :, 0:S] = total_d[:, yy * S : (yy + 1) * S]
                yb[yy, :, S:LANES] = jnp.zeros((F, LANES - S), bf16)
            for dy in range(1, Y):
                y_copy(dy).start()

    def y_total():
        out = yb[y].astype(f32)
        for dy in range(1, Y):
            out = out + yr[dy - 1].astype(f32)
        return out

    def lp_copy(d, s_tok, s_x):
        peer = lax.rem(me + d, ND)
        ref = lp.at[s_tok, s_x]
        return pltpu.make_async_remote_copy(
            ref,
            ref,
            ps_sem.at[d],
            pr_sem.at[s_tok, s_x],
            device_id=(peer // NV, peer % NV),
            device_id_type=MESH,
        )

    def lora_send():
        @pl.when(z == Z - 1)
        def _():
            for dy in range(1, Y):
                y_copy(dy).wait_recv()
            piece = y_total()[FW : FW + LR, :]
            lp[tok, x, 0:LR, :] = piece.astype(bf16)
            if lp.shape[2] > LR:
                lp[tok, x, LR:, :] = jnp.zeros((lp.shape[2] - LR, LANES), bf16)

            @pl.loop(1, ND)
            def _(d):
                lp_copy(d, tok, x).start()

    for i in range(Z):
        product(i)
        a_copy(i).start()
        if i >= 1:
            stage_b(i - 1)
        if i >= 2:
            stage_c(i - 2)
        if i >= 3:
            stage_d(i - 3)
    stage_b(Z - 1)
    if Z >= 2:
        stage_c(Z - 2)
    if Z < 4:
        for i in range(max(0, Z - 3), Z - 1):
            stage_d(i)
    else:
        stage_d(Z - 3)
    lora_send()
    stage_c(Z - 1)
    if Z >= 4:
        stage_d(Z - 2)
    stage_d(Z - 1)

    @pl.when(z != Z - 1)
    def _():
        for dy in range(1, Y):
            y_copy(dy).wait_recv()

    for s_tok in range(NT):
        for s_x in range(X):

            @pl.when(me != s_tok * NV + (Z - 1) * X + s_x)
            def _(s_tok=s_tok, s_x=s_x):
                lp_copy(1, s_tok, s_x).wait_recv()

    pieces = []
    for cc in range(CORES):
        for yy in range(Y):
            pieces.append(
                jnp.concatenate(
                    [lp[yy * CORES + cc, s_x].astype(f32)[0:LR, 0:S] for s_x in range(X)], axis=0
                )
            )
    lora_grad_t = jnp.concatenate(pieces, axis=1).astype(bf16)
    adg_out[...] = dot_nn(lora_grad_t, xa[:, 0:D])
    my_lora_t = jnp.concatenate(
        [lp[tok, s_x].astype(f32)[0:LR, 0:S] for s_x in range(X)], axis=0
    ).astype(bf16)
    slots = y_total()[0:FW, 0:S] + dot_nn(adloc[...], my_lora_t)
    hg_out[...] = dot_nn(slots.astype(bf16), pick_b).astype(bf16)

    for i in range(nk):
        for dy in range(1, Y):
            x_direct(i, dy).wait_send()
            x_copy(i, Y - 1 + dy, y_from(dy), core, sib).wait_send()
        x_copy(i, 0, y, core, sib).wait_send()
    for d in range(1, NT):
        lab_copy(d, y, core, lax.rem(tok + d, NT)).wait_send()

    @pl.loop(1, ND)
    def _(d):
        st_copy(d, me).wait_send()

    for i in range(Z):
        a_copy(i).wait_send()
        for dx in range(1, X):
            b_copy(i, dx).wait_send()

        @pl.when(z != order[i])
        def _(i=i):
            c_copy(i, lax.rem(z + Z - order[i], Z) - 1).wait_send()

    for dy in range(1, Y):
        y_copy(dy).wait_send()

    @pl.when(z == Z - 1)
    def _():
        @pl.loop(1, ND)
        def _(d):
            lp_copy(d, tok, x).wait_send()


def up(n, m):
    return -(-n // m) * m


def on_device(hidden, weight, adapter_down, adapter_up, targets, segment, response, chosen_first, reference_logp):
    NT = lax.axis_size("tok")
    NV = lax.axis_size("voc")
    ND = NT * NV
    Z = Z_CHIPS
    X, Y = NV // Z, NT // CORES
    rows, D = hidden.shape
    S = rows // 2
    V = weight.shape[1]
    K = adapter_down.shape[1]
    R = NT * S
    FW = D // NV
    LR = K // X
    F = up(FW + LR, 16)
    half = Y * S
    dpad = up(D, LANES)
    nk = len(range(0, D, KSTEP))
    cfg = (NT, NV, X, Y, Z, S, V, D, K)
    adloc = lax.dynamic_slice_in_dim(adapter_down, lax.axis_index("voc") * FW, FW, 0)
    vm = pl.BlockSpec(memory_space=pltpu.VMEM)
    hbm = pl.BlockSpec(memory_space=pl.ANY)
    dma = pltpu.SemaphoreType.DMA
    ratio, hg_t, adg_t, aug = pl.pallas_call(
        functools.partial(kernel, cfg),
        out_shape=(
            jax.ShapeDtypeStruct((1, reference_logp.shape[0]), f32),
            jax.ShapeDtypeStruct((FW, rows), bf16),
            jax.ShapeDtypeStruct((K, D), f32),
            jax.ShapeDtypeStruct((K, V), f32),
        ),
        in_specs=[vm, hbm, vm, vm, hbm, vm, vm, vm, vm, vm],
        out_specs=(vm, vm, vm, vm),
        scratch_shapes=[
            pltpu.VMEM((D + K, V), bf16),
            pltpu.VMEM((R, V), f32),
            pltpu.VMEM((R, V), bf16),
            pltpu.VMEM((R, dpad), bf16),
            pltpu.VMEM((R, up(KSTEP + K, LANES)), bf16),
            pltpu.VMEM((R, LANES), jnp.int32),
            pltpu.VMEM((ND, up(3 * R // LANES, 8), LANES), f32),
            pltpu.VMEM((R, LANES), f32),
            pltpu.VMEM((R, LANES), f32),
            pltpu.VMEM((R, LANES), f32),
            pltpu.VMEM((X * FW + K, R), f32),
            pltpu.VMEM((Z, X, F, R), bf16),
            pltpu.VMEM((Z, X, F, half), bf16),
            pltpu.VMEM((Z, X, F, half), bf16),
            pltpu.VMEM((Z, max(X - 1, 1), F, half), bf16),
            pltpu.VMEM((Z, F, half), bf16),
            pltpu.VMEM((Z - 1, F, half), bf16),
            pltpu.VMEM((Y, F, LANES), bf16),
            pltpu.VMEM((max(Y - 1, 1), F, LANES), bf16),
            pltpu.VMEM((NT, X, up(LR, 16), LANES), bf16),
            dma((nk + 1,)),
            dma((nk, 2 * Y)),
            dma((nk, 2 * Y)),
            dma((NT,)),
            dma((NT,)),
            dma((ND,)),
            dma((ND,)),
            dma((Z,)),
            dma((Z,)),
            dma((Z, X)),
            dma((Z, X)),
            dma((Z,)),
            dma((Z,)),
            dma((Y,)),
            dma((Y,)),
            dma((ND,)),
            dma((NT, X)),
        ],
        compiler_params=pltpu.CompilerParams(
            collective_id=0, has_side_effects=True, vmem_limit_bytes=62 * 1024 * 1024
        ),
    )(
        hidden.T,
        weight,
        adapter_down.T,
        adloc,
        adapter_up,
        targets.reshape(1, -1),
        segment.reshape(1, -1),
        response.reshape(1, -1),
        chosen_first.reshape(1, -1),
        reference_logp.reshape(1, -1),
    )
    return ratio.reshape(-1), hg_t.T, adg_t.T, aug


def solution(mesh):
    in_specs = (
        P("tok", None),
        P(None, ("tok", "voc")),
        P(),
        P(None, ("tok", "voc")),
        P("tok"),
        P("tok"),
        P("tok"),
        P(),
        P(),
    )
    out_specs = (P(), P("tok", "voc"), P(), P(None, ("tok", "voc")))
    return jax.shard_map(
        on_device, mesh=mesh, in_specs=in_specs, out_specs=out_specs, check_vma=False
    )
```

```python
import functools

import jax
import jax.numpy as jnp
from jax import lax
from jax.experimental import pallas as pl
from jax.experimental.pallas import tpu as pltpu
from jax.sharding import PartitionSpec as P

MESH = pl.DeviceIdType.MESH
f32 = jnp.float32
bf16 = jnp.bfloat16
adapter_scale = 2.0
target_margin = 10.0
CORES = 2
Z_CHIPS = 4
KSTEP = 1024
NSTEP_MAX = 2048
VSTEP_MAX = 3072
LANES = 128


def fit(step, limit):
    while step > limit:
        step //= 2
    return step


def dot_nn(a, b):
    return lax.dot_general(a, b, (((1,), (0,)), ((), ())), preferred_element_type=f32)


def dot_nt(a, b):
    return lax.dot_general(a, b, (((1,), (1,)), ((), ())), preferred_element_type=f32)


def dot_tn(a, b):
    return lax.dot_general(a, b, (((0,), (0,)), ((), ())), preferred_element_type=f32)


def eye_mask(n):
    return lax.broadcasted_iota(jnp.int32, (n, n), 0) == lax.broadcasted_iota(jnp.int32, (n, n), 1)


def to_col(row):
    n = row.shape[1]
    return jnp.sum(jnp.where(eye_mask(n), jnp.broadcast_to(row, (n, n)), 0.0), axis=1, keepdims=True)


def to_row(col):
    n = col.shape[0]
    return jnp.sum(jnp.where(eye_mask(n), jnp.broadcast_to(col, (n, n)), 0.0), axis=0, keepdims=True)


def kernel(
    cfg,
    ht,
    w,
    adt,
    adloc,
    au,
    tgt,
    seg,
    rsp,
    cf,
    refl,
    lr_out,
    hg_out,
    adg_out,
    aug_out,
    wv,
    lg,
    probs,
    xa,
    xl,
    lab,
    st,
    mx,
    sm,
    tm,
    g,
    sb,
    ra,
    tb,
    rb,
    ub,
    rc,
    yb,
    yr,
    lp,
    w_sem,
    xs_sem,
    xr_sem,
    ls_sem,
    lr_sem,
    ss_sem,
    sr_sem,
    as_sem,
    ar_sem,
    bs_sem,
    br_sem,
    cs_sem,
    cr_sem,
    ys_sem,
    yr_sem,
    ps_sem,
    pr_sem,
):
    NT, NV, X, Y, Z, S, V, D, K = cfg
    NSTEP, VSTEP = fit(NSTEP_MAX, V), fit(VSTEP_MAX, V)
    ND = NT * NV
    R = NT * S
    half = Y * S
    FW = D // NV
    LR = K // X
    tok = lax.axis_index("tok")
    voc = lax.axis_index("voc")
    y, core = tok // CORES, tok % CORES
    z, x = voc // X, voc % X
    me = tok * NV + voc
    sib = y * CORES + (1 - core)
    kst = list(range(0, D, KSTEP))
    nk = len(kst)
    dpad = xa.shape[1]

    def w_copy(i):
        size = min(KSTEP, D - kst[i])
        return pltpu.make_async_copy(
            w.at[pl.ds(kst[i], size), :], wv.at[pl.ds(kst[i], size), :], w_sem.at[i]
        )

    au_copy = pltpu.make_async_copy(au, wv.at[pl.ds(D, K), :], w_sem.at[nk])
    for i in range(nk):
        w_copy(i).start()
    au_copy.start()

    barrier = pltpu.get_barrier_semaphore()

    @pl.loop(1, ND)
    def _(d):
        peer = lax.rem(me + d, ND)
        pl.semaphore_signal(barrier, inc=1, device_id=(peer // NV, peer % NV), device_id_type=MESH)

    rows = ht.shape[1]
    resp = rsp[...]
    tri = (
        lax.broadcasted_iota(jnp.int32, (rows, rows), 0)
        <= lax.broadcasted_iota(jnp.int32, (rows, rows), 1)
    ).astype(bf16)
    before = dot_nn(jnp.broadcast_to(resp.astype(f32), (8, rows)).astype(bf16), tri)[0:1, :]
    position = before.astype(jnp.int32) - 1
    pick = (position == lax.broadcasted_iota(jnp.int32, (S, rows), 0)) & (resp > 0)
    pick_b = pick.astype(f32).astype(bf16)
    myrow = pl.multiple_of(core * half + y * S, S)
    xa[pl.ds(myrow, S), 0:D] = dot_nt(pick_b, ht[...]).astype(bf16)
    if dpad > D:
        xa[pl.ds(myrow, S), D:dpad] = jnp.zeros((S, dpad - D), bf16)
    lane = lax.broadcasted_iota(jnp.int32, (S, LANES), 1)
    t_col = jnp.sum(jnp.where(pick, tgt[...], 0), axis=1, keepdims=True)
    s_col = jnp.sum(jnp.where(pick, seg[...], 0), axis=1, keepdims=True)
    l_col = jnp.sum(jnp.where(pick, 1, 0), axis=1, keepdims=True)
    lab[pl.ds(myrow, S), :] = jnp.where(
        lane == 0, t_col, jnp.where(lane == 1, s_col, jnp.where(lane == 2, l_col, 0))
    )

    pl.semaphore_wait(barrier, ND - 1)

    def x_ref(i, yy, cc):
        size = min(KSTEP, dpad - kst[i])
        r0 = pl.multiple_of(cc * half + yy * S, S)
        return xa.at[pl.ds(r0, S), pl.ds(kst[i], size)]

    def x_copy(i, slot, yy, cc, dev):
        ref = x_ref(i, yy, cc)
        return pltpu.make_async_remote_copy(
            ref, ref, xs_sem.at[i, slot], xr_sem.at[i, slot], device_id=(dev, voc), device_id_type=MESH
        )

    def x_direct(i, dy):
        return x_copy(i, dy, y, core, lax.rem(y + dy, Y) * CORES + core)

    def x_recv(i, slot, yy, cc):
        return x_copy(i, slot, yy, cc, sib)

    def lab_copy(slot, yy, cc, dev):
        r0 = pl.multiple_of(cc * half + yy * S, S)
        ref = lab.at[pl.ds(r0, S), :]
        return pltpu.make_async_remote_copy(
            ref, ref, ls_sem.at[slot], lr_sem.at[slot], device_id=(dev, voc), device_id_type=MESH
        )

    for i in range(nk):
        for dy in range(1, Y):
            x_direct(i, dy).start()
        x_copy(i, 0, y, core, sib).start()
    for d in range(1, NT):
        lab_copy(d, y, core, lax.rem(tok + d, NT)).start()

    def y_from(dy):
        return lax.rem(y + Y - dy, Y)

    def forward(i):
        for dy in range(1, Y):
            x_recv(i, dy, y_from(dy), core).wait_recv()
            x_copy(i, Y - 1 + dy, y_from(dy), core, sib).start()

    def arrive(i):
        x_recv(i, 0, y, 1 - core).wait_recv()
        for dy in range(1, Y):
            x_recv(i, Y - 1 + dy, y_from(dy), 1 - core).wait_recv()

    nfull = V // NSTEP
    vtail = V - nfull * NSTEP
    mx[...] = jnp.full(mx.shape, -jnp.inf, f32)
    sm[...] = jnp.zeros(sm.shape, f32)
    tm[...] = jnp.zeros(tm.shape, f32)

    def folded(tile, op):
        out = tile[:, 0:LANES]
        for j in range(1, NSTEP // LANES):
            out = op(out, tile[:, j * LANES : (j + 1) * LANES])
        return out

    forward(0)
    tail_max = None
    for i in range(nk):
        last = i == nk - 1
        if not last:
            forward(i + 1)
        arrive(i)
        w_copy(i).wait()
        if last:
            size = D - kst[i]
            au_copy.wait()
            acc = dot_nt(xa[:, 0:D], adt[...])
            xl[:, 0:size] = xa[:, kst[i] : D]
            xl[:, size : size + K] = (adapter_scale * acc.astype(bf16).astype(f32)).astype(bf16)
            lhs = xl
            lcols = slice(0, size + K)
            wrows = slice(kst[i], D + K)
        else:
            lhs = xa
            lcols = slice(kst[i], kst[i] + KSTEP)
            wrows = slice(kst[i], kst[i] + KSTEP)

        def step(n, carry, i=i, last=last, lhs=lhs, lcols=lcols, wrows=wrows):
            cols = pl.ds(pl.multiple_of(n * NSTEP, NSTEP), NSTEP)
            tile = dot_nn(lhs[:, lcols], wv[wrows, cols])
            if i > 0:
                tile = tile + lg[:, cols]
            lg[:, cols] = tile
            if last:
                mx[...] = jnp.maximum(mx[...], folded(tile, jnp.maximum))
            return carry

        lax.fori_loop(0, nfull, step, 0)
        if vtail:
            cols = slice(nfull * NSTEP, V)
            tile = dot_nn(lhs[:, lcols], wv[wrows, cols])
            if i > 0:
                tile = tile + lg[:, cols]
            lg[:, cols] = tile
            if last:
                tail_max = jnp.max(tile, axis=1, keepdims=True)

    peak = jnp.max(mx[...], axis=1, keepdims=True)
    if vtail:
        peak = jnp.maximum(peak, tail_max)

    for d in range(1, NT):
        src = lax.rem(tok + NT - d, NT)
        lab_copy(d, src // CORES, src % CORES, sib).wait_recv()
    labels = lab[...]
    target = labels[:, 0:1]
    segs = labels[:, 1:2]
    live = labels[:, 2:3].astype(f32)
    slot_col = jnp.where(live > 0, target - me * V, -1)

    def exp_tile(cols, first, width):
        tile = lg[:, cols]
        hit = (lax.broadcasted_iota(jnp.int32, (R, width), 1) + first) == slot_col
        e = jnp.exp(tile - peak)
        lg[:, cols] = e
        return e, jnp.where(hit, tile, 0.0)

    def exp_step(n, carry):
        cols = pl.ds(pl.multiple_of(n * NSTEP, NSTEP), NSTEP)
        e, t = exp_tile(cols, n * NSTEP, NSTEP)
        sm[...] += folded(e, jnp.add)
        tm[...] += folded(t, jnp.add)
        return carry

    lax.fori_loop(0, nfull, exp_step, 0)
    summed = jnp.sum(sm[...], axis=1, keepdims=True)
    picked = jnp.sum(tm[...], axis=1, keepdims=True)
    if vtail:
        e, t = exp_tile(slice(nfull * NSTEP, V), nfull * NSTEP, vtail)
        summed = summed + jnp.sum(e, axis=1, keepdims=True)
        picked = picked + jnp.sum(t, axis=1, keepdims=True)

    nr = R // LANES
    st[pl.ds(me, 1)] = jnp.zeros((1,) + st.shape[1:], f32)
    for j, col in enumerate((peak, summed, picked)):
        for r in range(nr):
            st[me, j * nr + r : j * nr + r + 1, :] = to_row(col[r * LANES : (r + 1) * LANES, :])

    def st_copy(d, slot):
        peer = lax.rem(me + d, ND)
        return pltpu.make_async_remote_copy(
            st.at[slot],
            st.at[slot],
            ss_sem.at[d],
            sr_sem.at[d],
            device_id=(peer // NV, peer % NV),
            device_id_type=MESH,
        )

    @pl.loop(1, ND)
    def _(d):
        st_copy(d, me).start()

    @pl.loop(1, ND)
    def _(d):
        st_copy(d, lax.rem(me + ND - d, ND)).wait_recv()

    stats = st[...]
    m_all = stats[:, 0:nr, :]
    top = jnp.max(m_all, axis=0)
    total = jnp.sum(stats[:, nr : 2 * nr, :] * jnp.exp(m_all - top[None]), axis=0)
    hit_logit = jnp.sum(stats[:, 2 * nr : 3 * nr, :], axis=0)
    norm = top + jnp.log(total)
    logp = hit_logit - norm
    norm_col = jnp.concatenate([to_col(norm[r : r + 1, :]) for r in range(nr)], axis=0)
    logp_col = jnp.concatenate([to_col(logp[r : r + 1, :]) for r in range(nr)], axis=0)

    nseq = refl.shape[1]
    seq_lane = lax.broadcasted_iota(jnp.int32, (R, LANES), 1)
    mine = (segs == seq_lane) & (live > 0)
    counts = jnp.sum(jnp.where(mine, 1.0, 0.0), axis=0, keepdims=True)
    totals = jnp.sum(jnp.where(mine, logp_col, 0.0), axis=0, keepdims=True)
    counts = jnp.where(counts > 0, counts, 1.0)
    ratio = (totals / counts)[:, 0:nseq] - refl[...]
    lr_out[...] = ratio
    ratio_c = jnp.broadcast_to(ratio, (nseq, nseq))
    si = lax.broadcasted_iota(jnp.int32, (nseq, nseq), 0)
    sj = lax.broadcasted_iota(jnp.int32, (nseq, nseq), 1)
    ratio_col = jnp.sum(jnp.where(si == sj, ratio_c, 0.0), axis=1, keepdims=True)
    other = (si // 2 == sj // 2) & (si != sj)
    ratio_other = jnp.sum(jnp.where(other, jnp.broadcast_to(ratio_col, (nseq, nseq)), 0.0), axis=0, keepdims=True)
    npair = nseq // 2
    pi = lax.broadcasted_iota(jnp.int32, (npair, npair), 0)
    pj = lax.broadcasted_iota(jnp.int32, (npair, npair), 1)
    first_c = jnp.sum(
        jnp.where(pi == pj, jnp.broadcast_to(cf[...], (npair, npair)), 0), axis=1, keepdims=True
    )
    qi = lax.broadcasted_iota(jnp.int32, (npair, nseq), 0)
    qj = lax.broadcasted_iota(jnp.int32, (npair, nseq), 1)
    first = jnp.sum(jnp.where(qi == qj // 2, first_c, 0), axis=0, keepdims=True)
    even = (lax.broadcasted_iota(jnp.int32, (1, nseq), 1) % 2) == 0
    sign = jnp.where((first == 1) == even, 1.0, -1.0)
    margin = sign * (ratio - ratio_other)
    seq_weight = sign * 2.0 * (margin - target_margin) / counts[:, 0:nseq]
    member = (segs == lax.broadcasted_iota(jnp.int32, (R, nseq), 1)) & (live > 0)
    weight = jnp.sum(jnp.where(member, seq_weight, 0.0), axis=1, keepdims=True)
    scale = jnp.exp(peak - norm_col)

    size = D - kst[-1]
    lora = xl[:, size : size + K]
    eye_k = eye_mask(K).astype(f32).astype(bf16)
    lora_t = dot_nt(eye_k, lora).astype(bf16)

    def grad_tile(cols, first_col, width):
        hit = (lax.broadcasted_iota(jnp.int32, (R, width), 1) + first_col) == slot_col
        p = lg[:, cols] * scale
        gr = (weight * jnp.where(hit, p - 1.0, p)).astype(bf16)
        probs[:, cols] = gr
        aug_out[:, cols] = dot_nn(lora_t, gr)

    def grad_step(n, carry):
        grad_tile(pl.ds(pl.multiple_of(n * NSTEP, NSTEP), NSTEP), n * NSTEP, NSTEP)
        return carry

    lax.fori_loop(0, nfull, grad_step, 0)
    if vtail:
        grad_tile(slice(nfull * NSTEP, V), nfull * NSTEP, vtail)

    order = [Z - 1] + list(range(Z - 1))
    vfull = V // VSTEP
    ktail = V - vfull * VSTEP
    CH = X * FW
    F = sb.shape[2]
    keep = pl.multiple_of(core * half, LANES)
    give = pl.multiple_of((1 - core) * half, LANES)

    def product(i):
        q = order[i]
        extra = K if q == Z - 1 else 0
        r0, size = q * CH, CH + extra
        if ktail:
            g[0:size, :] = dot_nt(wv[r0 : r0 + size, vfull * VSTEP : V], probs[:, vfull * VSTEP : V])
        else:
            g[0:size, :] = jnp.zeros((size, R), f32)

        def body(n, carry):
            cols = pl.ds(pl.multiple_of(n * VSTEP, VSTEP), VSTEP)
            g[0:size, :] += dot_nt(wv[r0 : r0 + size, cols], probs[:, cols])
            return carry

        lax.fori_loop(0, vfull, body, 0)
        for xx in range(X):
            sb[i, xx, 0:FW, :] = g[xx * FW : (xx + 1) * FW, :].astype(bf16)
            if extra:
                sb[i, xx, FW : FW + LR, :] = (
                    adapter_scale * g[CH + xx * LR : CH + (xx + 1) * LR, :]
                ).astype(bf16)
                if F > FW + LR:
                    sb[i, xx, FW + LR : F, :] = jnp.zeros((F - FW - LR, R), bf16)
            elif F > FW:
                sb[i, xx, FW:F, :] = jnp.zeros((F - FW, R), bf16)

    def a_copy(i):
        return pltpu.make_async_remote_copy(
            sb.at[i, :, :, pl.ds(give, half)],
            ra.at[i],
            as_sem.at[i],
            ar_sem.at[i],
            device_id=(sib, voc),
            device_id_type=MESH,
        )

    def b_copy(i, dx):
        px = lax.rem(x + dx, X)
        return pltpu.make_async_remote_copy(
            tb.at[i, px],
            rb.at[i, dx - 1],
            bs_sem.at[i, dx],
            br_sem.at[i, dx],
            device_id=(tok, z * X + px),
            device_id_type=MESH,
        )

    def stage_b(i):
        a_copy(i).wait_recv()
        tb[i] = (sb[i, :, :, pl.ds(keep, half)].astype(f32) + ra[i].astype(f32)).astype(bf16)
        for dx in range(1, X):
            b_copy(i, dx).start()

    def c_copy(i, slot):
        return pltpu.make_async_remote_copy(
            ub.at[i],
            rc.at[slot],
            cs_sem.at[i],
            cr_sem.at[slot],
            device_id=(tok, order[i] * X + x),
            device_id_type=MESH,
        )

    def stage_c(i):
        q = order[i]
        total_c = tb[i, x].astype(f32)
        for dx in range(1, X):
            b_copy(i, dx).wait_recv()
            total_c = total_c + rb[i, dx - 1].astype(f32)
        ub[i] = total_c.astype(bf16)

        @pl.when(z != q)
        def _():
            c_copy(i, lax.rem(z + Z - q, Z) - 1).start()

    def y_copy(dy):
        py = lax.rem(y + dy, Y)
        return pltpu.make_async_remote_copy(
            yb.at[py],
            yr.at[dy - 1],
            ys_sem.at[dy],
            yr_sem.at[dy],
            device_id=(py * CORES + core, voc),
            device_id_type=MESH,
        )

    def stage_d(i):
        @pl.when(z == order[i])
        def _():
            total_d = ub[i].astype(f32)
            for j in range(Z - 1):
                pltpu.make_async_remote_copy(
                    ub.at[i],
                    rc.at[j],
                    cs_sem.at[i],
                    cr_sem.at[j],
                    device_id=(sib, voc),
                    device_id_type=MESH,
                ).wait_recv()
                total_d = total_d + rc[j].astype(f32)
            total_d = total_d.astype(bf16)
            for yy in range(Y):
                yb[yy, :, 0:S] = total_d[:, yy * S : (yy + 1) * S]
                yb[yy, :, S:LANES] = jnp.zeros((F, LANES - S), bf16)
            for dy in range(1, Y):
                y_copy(dy).start()

    def y_total():
        out = yb[y].astype(f32)
        for dy in range(1, Y):
            out = out + yr[dy - 1].astype(f32)
        return out

    def lp_copy(d, s_tok, s_x):
        peer = lax.rem(me + d, ND)
        ref = lp.at[s_tok, s_x]
        return pltpu.make_async_remote_copy(
            ref,
            ref,
            ps_sem.at[d],
            pr_sem.at[s_tok, s_x],
            device_id=(peer // NV, peer % NV),
            device_id_type=MESH,
        )

    def lora_send():
        @pl.when(z == Z - 1)
        def _():
            for dy in range(1, Y):
                y_copy(dy).wait_recv()
            piece = y_total()[FW : FW + LR, :]
            lp[tok, x, 0:LR, :] = piece.astype(bf16)
            if lp.shape[2] > LR:
                lp[tok, x, LR:, :] = jnp.zeros((lp.shape[2] - LR, LANES), bf16)

            @pl.loop(1, ND)
            def _(d):
                lp_copy(d, tok, x).start()

    for i in range(Z):
        product(i)
        a_copy(i).start()
        if i >= 1:
            stage_b(i - 1)
        if i >= 2:
            stage_c(i - 2)
        if i >= 3:
            stage_d(i - 3)
    stage_b(Z - 1)
    if Z >= 2:
        stage_c(Z - 2)
    if Z < 4:
        for i in range(max(0, Z - 3), Z - 1):
            stage_d(i)
    else:
        stage_d(Z - 3)
    lora_send()
    stage_c(Z - 1)
    if Z >= 4:
        stage_d(Z - 2)
    stage_d(Z - 1)

    @pl.when(z != Z - 1)
    def _():
        for dy in range(1, Y):
            y_copy(dy).wait_recv()

    for s_tok in range(NT):
        for s_x in range(X):

            @pl.when(me != s_tok * NV + (Z - 1) * X + s_x)
            def _(s_tok=s_tok, s_x=s_x):
                lp_copy(1, s_tok, s_x).wait_recv()

    pieces = []
    for cc in range(CORES):
        for yy in range(Y):
            pieces.append(
                jnp.concatenate(
                    [lp[yy * CORES + cc, s_x].astype(f32)[0:LR, 0:S] for s_x in range(X)], axis=0
                )
            )
    lora_grad_t = jnp.concatenate(pieces, axis=1).astype(bf16)
    adg_out[...] = dot_nn(lora_grad_t, xa[:, 0:D])
    my_lora_t = jnp.concatenate(
        [lp[tok, s_x].astype(f32)[0:LR, 0:S] for s_x in range(X)], axis=0
    ).astype(bf16)
    slots = y_total()[0:FW, 0:S] + dot_nn(adloc[...], my_lora_t)
    hg_out[...] = dot_nn(slots.astype(bf16), pick_b).astype(bf16)

    for i in range(nk):
        for dy in range(1, Y):
            x_direct(i, dy).wait_send()
            x_copy(i, Y - 1 + dy, y_from(dy), core, sib).wait_send()
        x_copy(i, 0, y, core, sib).wait_send()
    for d in range(1, NT):
        lab_copy(d, y, core, lax.rem(tok + d, NT)).wait_send()

    @pl.loop(1, ND)
    def _(d):
        st_copy(d, me).wait_send()

    for i in range(Z):
        a_copy(i).wait_send()
        for dx in range(1, X):
            b_copy(i, dx).wait_send()

        @pl.when(z != order[i])
        def _(i=i):
            c_copy(i, lax.rem(z + Z - order[i], Z) - 1).wait_send()

    for dy in range(1, Y):
        y_copy(dy).wait_send()

    @pl.when(z == Z - 1)
    def _():
        @pl.loop(1, ND)
        def _(d):
            lp_copy(d, tok, x).wait_send()


def up(n, m):
    return -(-n // m) * m


def on_device(hidden, weight, adapter_down, adapter_up, targets, segment, response, chosen_first, reference_logp):
    NT = lax.axis_size("tok")
    NV = lax.axis_size("voc")
    ND = NT * NV
    Z = Z_CHIPS
    X, Y = NV // Z, NT // CORES
    rows, D = hidden.shape
    S = rows // 2
    V = weight.shape[1]
    K = adapter_down.shape[1]
    R = NT * S
    FW = D // NV
    LR = K // X
    F = up(FW + LR, 16)
    half = Y * S
    dpad = up(D, LANES)
    nk = len(range(0, D, KSTEP))
    cfg = (NT, NV, X, Y, Z, S, V, D, K)
    adloc = lax.dynamic_slice_in_dim(adapter_down, lax.axis_index("voc") * FW, FW, 0)
    vm = pl.BlockSpec(memory_space=pltpu.VMEM)
    hbm = pl.BlockSpec(memory_space=pl.ANY)
    dma = pltpu.SemaphoreType.DMA
    ratio, hg_t, adg_t, aug = pl.pallas_call(
        functools.partial(kernel, cfg),
        out_shape=(
            jax.ShapeDtypeStruct((1, reference_logp.shape[0]), f32),
            jax.ShapeDtypeStruct((FW, rows), bf16),
            jax.ShapeDtypeStruct((K, D), f32),
            jax.ShapeDtypeStruct((K, V), f32),
        ),
        in_specs=[vm, hbm, vm, vm, hbm, vm, vm, vm, vm, vm],
        out_specs=(vm, vm, vm, vm),
        scratch_shapes=[
            pltpu.VMEM((D + K, V), bf16),
            pltpu.VMEM((R, V), f32),
            pltpu.VMEM((R, V), bf16),
            pltpu.VMEM((R, dpad), bf16),
            pltpu.VMEM((R, up(KSTEP + K, LANES)), bf16),
            pltpu.VMEM((R, LANES), jnp.int32),
            pltpu.VMEM((ND, up(3 * R // LANES, 8), LANES), f32),
            pltpu.VMEM((R, LANES), f32),
            pltpu.VMEM((R, LANES), f32),
            pltpu.VMEM((R, LANES), f32),
            pltpu.VMEM((X * FW + K, R), f32),
            pltpu.VMEM((Z, X, F, R), bf16),
            pltpu.VMEM((Z, X, F, half), bf16),
            pltpu.VMEM((Z, X, F, half), bf16),
            pltpu.VMEM((Z, max(X - 1, 1), F, half), bf16),
            pltpu.VMEM((Z, F, half), bf16),
            pltpu.VMEM((Z - 1, F, half), bf16),
            pltpu.VMEM((Y, F, LANES), bf16),
            pltpu.VMEM((max(Y - 1, 1), F, LANES), bf16),
            pltpu.VMEM((NT, X, up(LR, 16), LANES), bf16),
            dma((nk + 1,)),
            dma((nk, 2 * Y)),
            dma((nk, 2 * Y)),
            dma((NT,)),
            dma((NT,)),
            dma((ND,)),
            dma((ND,)),
            dma((Z,)),
            dma((Z,)),
            dma((Z, X)),
            dma((Z, X)),
            dma((Z,)),
            dma((Z,)),
            dma((Y,)),
            dma((Y,)),
            dma((ND,)),
            dma((NT, X)),
        ],
        compiler_params=pltpu.CompilerParams(
            collective_id=0, has_side_effects=True, vmem_limit_bytes=62 * 1024 * 1024
        ),
    )(
        hidden.T,
        weight,
        adapter_down.T,
        adloc,
        adapter_up,
        targets.reshape(1, -1),
        segment.reshape(1, -1),
        response.reshape(1, -1),
        chosen_first.reshape(1, -1),
        reference_logp.reshape(1, -1),
    )
    return ratio.reshape(-1), hg_t.T, adg_t.T, aug


def solution(mesh):
    in_specs = (
        P("tok", None),
        P(None, ("tok", "voc")),
        P(),
        P(None, ("tok", "voc")),
        P("tok"),
        P("tok"),
        P("tok"),
        P(),
        P(),
    )
    out_specs = (P(), P("tok", "voc"), P(), P(None, ("tok", "voc")))
    return jax.shard_map(
        on_device, mesh=mesh, in_specs=in_specs, out_specs=out_specs, check_vma=False
    )
```
